32 devices in a mesh: panel: 4 (over y, x), front: 8 (over z, core).
Axes of the slice: x: 2, y: 2, z: 4, core: 2. Of those that a mesh axis runs over, the one named last changes fastest.
Arguments:
- leaf_inv: float32 [4, 8, 768, 768], P('panel', 'front'), may hold values from -0.21875 to 0.21875
- parent_inv: float32 [4, 8, 768, 768], P('panel', 'front'), may hold values from -0.21875 to 0.21875
- up_coupling: float32 [4, 8, 384, 768], P('panel', 'front'), may hold values from -0.21875 to 0.21875
- down_coupling: float32 [4, 8, 768, 384], P('panel', 'front'), may hold values from -0.3125 to 0.3125
- interface_coupling: float32 [4, 8, 768, 512], P('panel', 'front'), may hold values from -0.25 to 0.25
- leaf_sources: float32 [4, 8, 3, 768, 128], P('panel', 'front'), may hold values from -6 to 6
- parent_sources: float32 [4, 8, 3, 768, 128], P('panel', 'front'), may hold values from -6 to 6
- parent_of: int32 [4, 8], P('panel'), may hold values from 0 to 7
- update_count: int32 [4, 8], P('panel'), may hold values from 128 to 384, as said below
- update_rows: int32 [4, 8, 384], P('panel'), may hold values from 0 to 767, as said below
Outputs:
- leaf_solution: float32 [4, 8, 3, 768, 128], P('panel', 'front')
- parent_solution: float32 [4, 8, 3, 768, 128], P('panel', 'front')
The draws below stay inside these ranges and needn't reach their ends.
Inputs may be any that keep to these rules, and one draw needn't show every extreme that they name: `update_count`: a multiple of 128; some leaf of every panel has 384. `update_rows`: the entries of one leaf are distinct; those at or past its update_count are padding.
All inputs are finite; a program needn't handle non-finite values.
Results may differ from the reference program's by a relative error of at most 0.0003.
Values sent between devices are 32-bit elements; how exact they have to be, the bound alone decides.
No kernel may reach another device: no remote copies, remote signals or barrier semaphores. Data moves between devices by JAX's collectives and lax.ppermute only.
A program may use at most 128 MiB of HBM per device.

```python
import math
import jax
import jax.numpy as jnp
import numpy as np
from jax import lax

LEAF = 768
PARENT = 768
BLOCK = 128
UPDATE_BLOCKS = 3
IFACE = 512
SOURCES = 128
TICKS = 3
UMAX = 384
N_PANEL = 4
N_FRONT = 8


def draw_update_count(key, part):
    first_key = jax.random.fold_in(key, 11)
    second_key = jax.random.fold_in(key, 12)
    blocks = jax.random.randint(first_key, (N_PANEL, N_FRONT), 1, UPDATE_BLOCKS + 1)
    fullest = jax.random.randint(second_key, (N_PANEL, 1), 0, N_FRONT)
    positions = jnp.arange(N_FRONT)[None, :]
    blocks = jnp.where(positions == fullest, UPDATE_BLOCKS, blocks)
    return (blocks * BLOCK).astype(jnp.int32)


def leading_rows(subkey):
    return jax.random.permutation(subkey, PARENT)[:UMAX]


def draw_update_rows(key, part):
    subkeys = jax.random.split(jax.random.fold_in(key, 21), N_PANEL * N_FRONT)
    chosen = jax.vmap(leading_rows)(subkeys)
    return chosen.reshape(N_PANEL, N_FRONT, UMAX).astype(jnp.int32)


def with_ends(result, own_key, least, largest):
    shape = result.shape
    place = [jax.random.randint(jax.random.fold_in(own_key, axis), (), 0, shape[axis]) for axis in range(len(shape))]
    result = result.at[tuple(place)].set(least)
    longest = shape.index(max(shape))
    place[longest] = (place[longest] + 1) % shape[longest]
    return result.at[tuple(place)].set(largest)


def shard_levels(key, shape, cuts, low, largest):
    def one(axis_at, parts):
        heights = jax.random.uniform(jax.random.fold_in(jax.random.fold_in(key, 6), axis_at), (parts,), jnp.float32, low / len(cuts), largest / len(cuts))
        return jnp.repeat(jnp.exp(heights), shape[axis_at] // parts).reshape((-1,) + (1,) * (len(shape) - axis_at - 1))

    factor_of = one(*cuts[0])
    for cut in cuts[1:]:
        factor_of = factor_of * one(*cut)
    return factor_of


def rank_bounds(count, lean):
    weights = [(1 << 20) // math.isqrt(rank ** lean) + 1 for rank in range(1, count + 1)]
    scale = 1 + sum(weights) // (1 << 30)
    return np.cumsum(np.array([max(1, weight // scale) for weight in weights]))


def skewed_ids(own_key, shape, number_of, skew):
    grid = rank_bounds(number_of, skew)
    ticket = jax.random.randint(jax.random.fold_in(own_key, 1), shape, 0, int(grid[number_of - 1]))
    rank = jnp.searchsorted(jnp.asarray(grid, jnp.int32), ticket, side="right")
    return jax.random.permutation(jax.random.fold_in(own_key, 2), number_of)[rank].astype(jnp.int32)


def gaussian(stream_key, dims, spread, bound, pieces=(), held_as=jnp.bfloat16):
    array = jax.random.normal(stream_key, dims, jnp.float32) * spread
    if len(pieces) > 0:
        array = shard_levels(stream_key, dims, pieces, -0.22, 0.18) * array
    return jnp.clip(array, min=-bound, max=bound).astype(held_as)


def setup_inputs(seed: int = 0) -> dict:
    arg_keys = jax.random.split(jax.random.key(seed), 11)
    leaf_inv = gaussian(arg_keys[0], (N_PANEL, N_FRONT, LEAF, LEAF), LEAF ** -0.5, 0.21875, ((0, 4), (1, 8)), jnp.float32)
    parent_inv = gaussian(arg_keys[1], (N_PANEL, N_FRONT, PARENT, PARENT), PARENT ** -0.5, 0.21875, ((0, 4), (1, 8)), jnp.float32)
    up_coupling = gaussian(arg_keys[2], (N_PANEL, N_FRONT, UMAX, LEAF), LEAF ** -0.5, 0.21875, ((0, 4), (1, 8)), jnp.float32)
    down_coupling = gaussian(arg_keys[3], (N_PANEL, N_FRONT, LEAF, UMAX), UMAX ** -0.5, 0.3125, ((0, 4), (1, 8)), jnp.float32)
    interface_coupling = gaussian(arg_keys[4], (N_PANEL, N_FRONT, LEAF, IFACE), IFACE ** -0.5, 0.25, ((0, 4), (1, 8)), jnp.float32)
    leaf_sources = gaussian(arg_keys[5], (N_PANEL, N_FRONT, TICKS, LEAF, SOURCES), 1.0, 6.0, ((0, 4), (1, 8)), jnp.float32)
    parent_sources = gaussian(arg_keys[6], (N_PANEL, N_FRONT, TICKS, PARENT, SOURCES), 1.0, 6.0, ((0, 4), (1, 8)), jnp.float32)
    parent_of = with_ends(skewed_ids(arg_keys[7], (N_PANEL, N_FRONT), N_FRONT, 2), jax.random.fold_in(arg_keys[7], 3), 0, N_FRONT - 1).astype(jnp.int32)
    update_count = draw_update_count(jax.random.fold_in(arg_keys[10], 71), 0)
    update_rows = draw_update_rows(jax.random.fold_in(arg_keys[10], 71), 0)
    return {"leaf_inv": leaf_inv, "parent_inv": parent_inv, "up_coupling": up_coupling, "down_coupling": down_coupling, "interface_coupling": interface_coupling, "leaf_sources": leaf_sources, "parent_sources": parent_sources, "parent_of": parent_of, "update_count": update_count, "update_rows": update_rows}


highest_precision = lax.Precision.HIGHEST


def apply_front(matrix, operand):
    return jnp.einsum("pfij,pfjb->pfib", matrix, operand, precision=highest_precision)


def assemble_panel(update, parents, counts, row_ids):
    fronts, update_cap, columns = update.shape
    live_slots = jnp.arange(update_cap, dtype=jnp.int32)[None, :] < counts[:, None]
    targets = jnp.where(live_slots, parents[:, None] * PARENT + row_ids, fronts * PARENT).astype(jnp.int32)
    summed = jax.ops.segment_sum(update.reshape(fronts * update_cap, columns), targets.reshape(-1), num_segments=fronts * PARENT + 1)
    return summed[:fronts * PARENT].reshape(fronts, PARENT, columns)


def descend_panel(solved, parents, counts, row_ids):
    fronts, parent_order, columns = solved.shape
    update_cap = row_ids.shape[1]
    flattened = solved.reshape(fronts * parent_order, columns)
    take_index = (parents[:, None] * parent_order + row_ids).reshape(-1).astype(jnp.int32)
    picked = jnp.take(flattened, take_index, axis=0).reshape(fronts, update_cap, columns)
    live_slots = jnp.arange(update_cap, dtype=jnp.int32)[None, :] < counts[:, None]
    return jnp.where(live_slots[:, :, None], picked, 0.0)


def reference(leaf_inv, parent_inv, up_coupling, down_coupling, interface_coupling, leaf_sources, parent_sources, parent_of, update_count, update_rows):
    live_slots = jnp.arange(UMAX, dtype=jnp.int32)[None, None, :] < update_count[:, :, None]
    previous = None
    leaf_list = []
    parent_list = []
    for tick_index in range(TICKS):
        sources = leaf_sources[:, :, tick_index]
        if tick_index == 0:
            leaf_rhs = sources
        else:
            edge = previous[:, :, LEAF - IFACE:, :]
            interface = jnp.concatenate([jnp.zeros_like(edge[:1]), edge[:-1]], axis=0)
            leaf_rhs = sources + apply_front(interface_coupling, interface)
        partial_solution = apply_front(leaf_inv, leaf_rhs)
        update = jnp.where(live_slots[..., None], apply_front(up_coupling, partial_solution), 0.0)
        assembled = jax.vmap(assemble_panel)(update, parent_of, update_count, update_rows)
        solved = apply_front(parent_inv, parent_sources[:, :, tick_index] - assembled)
        descended = jax.vmap(descend_panel)(solved, parent_of, update_count, update_rows)
        leaf_now = partial_solution - apply_front(down_coupling, descended)
        leaf_list.append(leaf_now)
        parent_list.append(solved)
        previous = leaf_now
    return jnp.stack(leaf_list, axis=2), jnp.stack(parent_list, axis=2)
```

```python
import functools

import jax
import jax.numpy as jnp
from jax import lax
from jax.experimental import pallas as pl
from jax.experimental.pallas import tpu as pltpu
from jax.sharding import PartitionSpec as P

TWIN = 1
VMEM_BYTES = 48 * 1024 * 1024


def swapped(value, mask):
    count = lax.axis_size("front")
    return lax.ppermute(value, "front", [(place, place ^ mask) for place in range(count)])


def onward(value, panel_step, mask):
    panels = lax.axis_size("panel")
    fronts = lax.axis_size("front")
    pairs = []
    for panel in range(panels):
        for place in range(fronts):
            goal = (panel + panel_step) % panels
            pairs.append((panel * fronts + place, goal * fronts + (place ^ mask)))
    return lax.ppermute(value, ("panel", "front"), pairs)


def cube_masks(count):
    masks = []
    low = 2
    while low < count:
        masks.append(2 * low - 2)
        low *= 2
    return masks[::-1]


def offsets(masks):
    held = [0]
    for mask in masks:
        held = held + [offset ^ mask for offset in held]
    return held


def spread(held, masks):
    held = dict(held)
    for mask in masks:
        held.update({offset ^ mask: swapped(value, mask) for offset, value in list(held.items())})
    return held


def delivered(parts, masks):
    parts = dict(parts)
    span = offsets(masks)
    first = None
    for step in range(len(masks) - 1, -1, -1):
        mask = masks[step]
        for offset in span[2 ** step - 1 :: -1]:
            received = swapped(parts.pop(offset ^ mask), mask)
            first = received if first is None else first
            parts[offset] = parts[offset] + received
    return parts[0], first


def product(matrix, operand):
    return jnp.dot(matrix, operand, precision=lax.Precision.HIGH, preferred_element_type=jnp.float32)


def prepared(matrix, operand):
    return jnp.dot(matrix, operand, precision=lax.Precision.HIGHEST, preferred_element_type=jnp.float32)


def halves(value):
    rounded = lax.reduce_precision(value, 8, 7)
    return rounded.astype(jnp.bfloat16), (value - rounded).astype(jnp.bfloat16)


def side_by_side(value):
    high = value.astype(jnp.bfloat16)
    low = (value - high.astype(jnp.float32)).astype(jnp.bfloat16)
    return jnp.concatenate([high, low], axis=1)


def summed(pair):
    columns = pair.shape[1] // 2
    return pair[:, :columns] + pair[:, columns:]


def after(value, event):
    return lax.optimization_barrier((value, event))[0]


def solve_kernel(offsets_in, place, parents, rows, high, low, sources, *refs):
    blocks, out, rhs = refs[:-2], refs[-2], refs[-1]
    rhs[...] = sources[...]
    extent = (rhs.shape[0], rows.shape[1])
    for offset, block in zip(offsets_in, blocks):
        leaf = place[0] ^ offset

        @pl.when(parents[0, leaf] == place[0])
        def _():
            choice = lax.broadcasted_iota(jnp.int32, extent, 0) == rows[pl.ds(leaf, 1), :]
            pair = jnp.dot(
                jnp.where(choice, 1.0, 0.0).astype(jnp.bfloat16),
                side_by_side(block[...]),
                preferred_element_type=jnp.float32,
            )
            rhs[...] -= summed(pair)

    both = side_by_side(rhs[...])
    columns = out.shape[1]
    out[...] = summed(jnp.dot(high[...], both, preferred_element_type=jnp.float32)) + jnp.dot(
        low[...], both[:, :columns], preferred_element_type=jnp.float32
    )


def parent_solve(place, parents, rows, high, low, sources, blocks):
    order = sources.shape[0]
    depth = sum(block.shape[0] for block in blocks.values())
    smem = pl.BlockSpec(memory_space=pltpu.SMEM)
    vmem = pl.BlockSpec(memory_space=pltpu.VMEM)
    return pl.pallas_call(
        functools.partial(solve_kernel, list(blocks)),
        out_shape=jax.ShapeDtypeStruct(sources.shape, jnp.float32),
        in_specs=[smem] * 2 + [vmem] * (4 + len(blocks)),
        out_specs=vmem,
        scratch_shapes=[pltpu.VMEM(sources.shape, jnp.float32)],
        compiler_params=pltpu.CompilerParams(vmem_limit_bytes=VMEM_BYTES),
        cost_estimate=pl.CostEstimate(
            flops=8 * order * order * sources.shape[1],
            bytes_accessed=4 * order * (order + 256) + 512 * depth,
            transcendentals=0,
        ),
        name="parent_solve",
    )(place, parents, rows, high, low, sources, *blocks.values())


def rows_kernel(offsets_out, place, parents, counts, rows, own, other, *refs):
    outs, wide = refs[:-1], refs[-1]
    wide[0] = side_by_side(own[...])
    wide[1] = side_by_side(other[...])
    cap = rows.shape[1]
    order = own.shape[0]
    lanes = 128
    for offset, out in zip(offsets_out, outs):
        leaf = place[0] ^ offset
        parent = parents[0, leaf]
        mine = parent == place[0]
        here = mine | (parent == (place[0] ^ TWIN))

        @pl.when(jnp.logical_not(here))
        def _():
            out[...] = jnp.zeros_like(out)

        @pl.when(here)
        def _():
            slot = lax.broadcasted_iota(jnp.int32, (lanes, cap), 1)
            column = jnp.where(slot < counts[0, leaf], jnp.broadcast_to(rows[pl.ds(leaf, 1), :], (lanes, cap)), -1).T
            lane = lax.broadcasted_iota(jnp.int32, (cap, lanes), 1)
            choice = jnp.concatenate(
                [jnp.where(column == lane + start, 1.0, 0.0).astype(jnp.bfloat16) for start in range(0, order, lanes)],
                axis=1,
            )
            out[...] = summed(
                jnp.dot(choice, wide[jnp.where(mine, 0, 1)], preferred_element_type=jnp.float32)
            )


def parent_rows(place, parents, counts, rows, own, other, wanted):
    cap = rows.shape[1]
    order, columns = own.shape
    smem = pl.BlockSpec(memory_space=pltpu.SMEM)
    vmem = pl.BlockSpec(memory_space=pltpu.VMEM)
    found = pl.pallas_call(
        functools.partial(rows_kernel, wanted),
        out_shape=[jax.ShapeDtypeStruct((cap, columns), jnp.float32)] * len(wanted),
        in_specs=[smem] * 3 + [vmem] * 3,
        out_specs=[vmem] * len(wanted),
        scratch_shapes=[pltpu.VMEM((2, order, 2 * columns), jnp.bfloat16)],
        compiler_params=pltpu.CompilerParams(vmem_limit_bytes=VMEM_BYTES),
        cost_estimate=pl.CostEstimate(
            flops=4 * cap * order * columns * len(wanted), bytes_accessed=8 * order * columns, transcendentals=0
        ),
        name="parent_rows",
    )(place, parents, counts, rows, own, other)
    return dict(zip(wanted, found))


def local(
    leaf_inv,
    parent_inv,
    up_coupling,
    down_coupling,
    interface_coupling,
    leaf_sources,
    parent_sources,
    parent_of,
    update_count,
    update_rows,
):
    inverse = leaf_inv[0, 0]
    upward = up_coupling[0, 0]
    downward = down_coupling[0, 0]
    coupling = interface_coupling[0, 0]
    ticks = leaf_sources.shape[2]
    columns = leaf_sources.shape[4]
    leaf_order = inverse.shape[0]
    iface_rows = coupling.shape[1]
    row_ids = update_rows[0]
    fronts = lax.axis_size("front")
    panels = lax.axis_size("panel")
    myself = lax.axis_index("front")
    place = myself.astype(jnp.int32).reshape(1)
    masks = cube_masks(fronts)
    span = offsets(masks)
    own_count = lax.dynamic_index_in_dim(update_count[0], myself, 0, keepdims=False)
    own_live = (jnp.arange(row_ids.shape[1], dtype=jnp.int32) < own_count)[:, None]

    def edge(value):
        return value[leaf_order - iface_rows :]

    sources = leaf_sources[0, 0]
    partial_solution = product(inverse, sources[0])
    update = jnp.where(own_live, product(upward, partial_solution), 0.0)
    held = spread({0: update}, masks)
    parent_high, parent_low = halves(parent_inv[0, 0])

    later = jnp.concatenate([sources[tick] for tick in range(1, ticks)], axis=1)
    along = jnp.where(own_live, prepared(upward, inverse), 0.0)
    through = jnp.where(lax.axis_index("panel") > 0, prepared(along, coupling), 0.0)
    next_through = onward(through, -1, 0)
    next_sources = onward(product(along, later), -1, 0)
    next_descended = prepared(next_through, edge(downward))
    own_later = product(inverse, later)

    leaf_list = []
    parent_list = []
    interface = None
    for tick in range(ticks):
        blocks = {offset: held[offset] for offset in span}
        blocks.update({offset ^ TWIN: swapped(held[offset], TWIN) for offset in span})
        solved = parent_solve(
            place, parent_of, row_ids, parent_high, parent_low, parent_sources[0, 0, tick], blocks
        )
        parent_list.append(solved)
        parts = parent_rows(place, parent_of, update_count, row_ids, solved, swapped(solved, TWIN), span)
        descended, first = delivered(parts, masks)
        at = slice((tick - 1) * columns, tick * columns)
        if tick > 0:
            arrived = after(interface, first)
            partial_solution = own_later[:, at] + product(inverse, product(coupling, arrived))
        if tick + 1 < ticks:
            at = slice(tick * columns, (tick + 1) * columns)
            base = next_sources[:, at] + product(next_through, edge(partial_solution))
            update = base - product(next_descended, descended)
            moved = onward(update, 1, 0)
            held = spread({0: moved, masks[0]: onward(update, 1, masks[0])}, masks[1:])
            leaf_now = partial_solution - product(downward, after(descended, moved))
            interface = lax.ppermute(edge(leaf_now), "panel", [(spot, spot + 1) for spot in range(panels - 1)])
        else:
            leaf_now = partial_solution - product(downward, descended)
        leaf_list.append(leaf_now)
    leaf_out = jnp.stack(leaf_list, axis=0)[None, None]
    parent_out = jnp.stack(parent_list, axis=0)[None, None]
    return (leaf_out, parent_out)


def solution(mesh):
    placed = (
        P("panel", "front", None, None),
        P("panel", "front", None, None),
        P("panel", "front", None, None),
        P("panel", "front", None, None),
        P("panel", "front", None, None),
        P("panel", "front", None, None, None),
        P("panel", "front", None, None, None),
        P("panel", None),
        P("panel", None),
        P("panel", None, None),
    )
    return jax.shard_map(
        local,
        mesh=mesh,
        in_specs=placed,
        out_specs=(P("panel", "front", None, None, None), P("panel", "front", None, None, None)),
        check_vma=False,
    )
```

```python
import functools

import jax
import jax.numpy as jnp
from jax import lax
from jax.experimental import pallas as pl
from jax.experimental.pallas import tpu as pltpu
from jax.sharding import PartitionSpec as P

TWIN = 1
VMEM_BYTES = 48 * 1024 * 1024


def swapped(value, mask):
    count = lax.axis_size("front")
    return lax.ppermute(value, "front", [(place, place ^ mask) for place in range(count)])


def onward(value, panel_step, mask):
    panels = lax.axis_size("panel")
    fronts = lax.axis_size("front")
    pairs = []
    for panel in range(panels):
        for place in range(fronts):
            goal = (panel + panel_step) % panels
            pairs.append((panel * fronts + place, goal * fronts + (place ^ mask)))
    return lax.ppermute(value, ("panel", "front"), pairs)


def cube_masks(count):
    masks = []
    low = 2
    while low < count:
        masks.append(2 * low - 2)
        low *= 2
    return masks[::-1]


def offsets(masks):
    held = [0]
    for mask in masks:
        held = held + [offset ^ mask for offset in held]
    return held


def spread(held, masks):
    held = dict(held)
    for mask in masks:
        held.update({offset ^ mask: swapped(value, mask) for offset, value in list(held.items())})
    return held


def delivered(parts, masks):
    parts = dict(parts)
    span = offsets(masks)
    for step in range(len(masks) - 1, -1, -1):
        mask = masks[step]
        for offset in span[2 ** step - 1 :: -1]:
            parts[offset] = parts[offset] + swapped(parts.pop(offset ^ mask), mask)
    return parts[0]


def product(matrix, operand):
    return jnp.dot(matrix, operand, precision=lax.Precision.HIGH, preferred_element_type=jnp.float32)


def halves(value):
    rounded = lax.reduce_precision(value, 8, 7)
    return rounded.astype(jnp.bfloat16), (value - rounded).astype(jnp.bfloat16)


def side_by_side(value):
    high = value.astype(jnp.bfloat16)
    low = (value - high.astype(jnp.float32)).astype(jnp.bfloat16)
    return jnp.concatenate([high, low], axis=1)


def summed(pair):
    columns = pair.shape[1] // 2
    return pair[:, :columns] + pair[:, columns:]


def after(value, event):
    return lax.optimization_barrier((value, event))[0]


def subtract_rows(rhs, offsets_in, blocks, place, parents, counts, rows):
    cap = rows.shape[1]
    extent = (rhs.shape[0], cap)
    for offset, block in zip(offsets_in, blocks):
        leaf = place[0] ^ offset

        @pl.when(parents[0, leaf] == place[0])
        def _():
            slot = lax.broadcasted_iota(jnp.int32, (1, cap), 1)
            targets = jnp.where(slot < counts[0, leaf], rows[pl.ds(leaf, 1), :], -1)
            choice = lax.broadcasted_iota(jnp.int32, extent, 0) == targets
            pair = jnp.dot(
                jnp.where(choice, 1.0, 0.0).astype(jnp.bfloat16),
                side_by_side(block[...]),
                preferred_element_type=jnp.float32,
            )
            rhs[...] -= summed(pair)


def early_kernel(offsets_in, tick, place, parents, counts, rows, sources, *refs):
    blocks, rhs = refs[:-1], refs[-1]
    rhs[...] = sources[tick]
    subtract_rows(rhs, offsets_in, blocks, place, parents, counts, rows)


def solve_kernel(offsets_in, place, parents, counts, rows, high, low, partial_rhs, *refs):
    blocks, out, rhs = refs[:-2], refs[-2], refs[-1]
    rhs[...] = partial_rhs[...]
    subtract_rows(rhs, offsets_in, blocks, place, parents, counts, rows)
    both = side_by_side(rhs[...])
    columns = out.shape[1]
    out[...] = summed(jnp.dot(high[...], both, preferred_element_type=jnp.float32)) + jnp.dot(
        low[...], both[:, :columns], preferred_element_type=jnp.float32
    )


def rows_subtracted(place, parents, counts, rows, sources, tick, blocks):
    smem = pl.BlockSpec(memory_space=pltpu.SMEM)
    vmem = pl.BlockSpec(memory_space=pltpu.VMEM)
    order, columns = sources.shape[1:]
    return pl.pallas_call(
        functools.partial(early_kernel, list(blocks), tick),
        out_shape=jax.ShapeDtypeStruct((order, columns), jnp.float32),
        in_specs=[smem] * 3 + [vmem] * (2 + len(blocks)),
        out_specs=vmem,
        compiler_params=pltpu.CompilerParams(vmem_limit_bytes=VMEM_BYTES),
        cost_estimate=pl.CostEstimate(
            flops=4 * order * rows.shape[1] * columns * len(blocks),
            bytes_accessed=8 * order * columns,
            transcendentals=0,
        ),
        name="rows_subtracted",
    )(place, parents, counts, rows, sources, *blocks.values())


def parent_solve(place, parents, counts, rows, high, low, partial_rhs, blocks):
    order, columns = partial_rhs.shape
    smem = pl.BlockSpec(memory_space=pltpu.SMEM)
    vmem = pl.BlockSpec(memory_space=pltpu.VMEM)
    return pl.pallas_call(
        functools.partial(solve_kernel, list(blocks)),
        out_shape=jax.ShapeDtypeStruct(partial_rhs.shape, jnp.float32),
        in_specs=[smem] * 3 + [vmem] * (4 + len(blocks)),
        out_specs=vmem,
        scratch_shapes=[pltpu.VMEM(partial_rhs.shape, jnp.float32)],
        compiler_params=pltpu.CompilerParams(vmem_limit_bytes=VMEM_BYTES),
        cost_estimate=pl.CostEstimate(
            flops=8 * order * order * columns, bytes_accessed=4 * order * (order + 256), transcendentals=0
        ),
        name="parent_solve",
    )(place, parents, counts, rows, high, low, partial_rhs, *blocks.values())


def rows_kernel(offsets_out, place, parents, counts, rows, own, other, *refs):
    outs, wide = refs[:-1], refs[-1]
    wide[0] = side_by_side(own[...])
    wide[1] = side_by_side(other[...])
    cap = rows.shape[1]
    order = own.shape[0]
    lanes = 128
    for offset, out in zip(offsets_out, outs):
        leaf = place[0] ^ offset
        parent = parents[0, leaf]
        mine = parent == place[0]
        here = mine | (parent == (place[0] ^ TWIN))

        @pl.when(jnp.logical_not(here))
        def _():
            out[...] = jnp.zeros_like(out)

        @pl.when(here)
        def _():
            slot = lax.broadcasted_iota(jnp.int32, (lanes, cap), 1)
            column = jnp.where(slot < counts[0, leaf], jnp.broadcast_to(rows[pl.ds(leaf, 1), :], (lanes, cap)), -1).T
            lane = lax.broadcasted_iota(jnp.int32, (cap, lanes), 1)
            choice = jnp.concatenate(
                [jnp.where(column == lane + start, 1.0, 0.0).astype(jnp.bfloat16) for start in range(0, order, lanes)],
                axis=1,
            )
            out[...] = summed(
                jnp.dot(choice, wide[jnp.where(mine, 0, 1)], preferred_element_type=jnp.float32)
            )


def parent_rows(place, parents, counts, rows, own, other, wanted):
    cap = rows.shape[1]
    order, columns = own.shape
    smem = pl.BlockSpec(memory_space=pltpu.SMEM)
    vmem = pl.BlockSpec(memory_space=pltpu.VMEM)
    found = pl.pallas_call(
        functools.partial(rows_kernel, wanted),
        out_shape=[jax.ShapeDtypeStruct((cap, columns), jnp.float32)] * len(wanted),
        in_specs=[smem] * 3 + [vmem] * 3,
        out_specs=[vmem] * len(wanted),
        scratch_shapes=[pltpu.VMEM((2, order, 2 * columns), jnp.bfloat16)],
        compiler_params=pltpu.CompilerParams(vmem_limit_bytes=VMEM_BYTES),
        cost_estimate=pl.CostEstimate(
            flops=4 * cap * order * columns * len(wanted), bytes_accessed=8 * order * columns, transcendentals=0
        ),
        name="parent_rows",
    )(place, parents, counts, rows, own, other)
    return dict(zip(wanted, found))


def local(
    leaf_inv,
    parent_inv,
    up_coupling,
    down_coupling,
    interface_coupling,
    leaf_sources,
    parent_sources,
    parent_of,
    update_count,
    update_rows,
):
    inverse = leaf_inv[0, 0]
    upward = up_coupling[0, 0]
    downward = down_coupling[0, 0]
    coupling = interface_coupling[0, 0]
    ticks = leaf_sources.shape[2]
    columns = leaf_sources.shape[4]
    leaf_order = inverse.shape[0]
    iface_rows = coupling.shape[1]
    row_ids = update_rows[0]
    fronts = lax.axis_size("front")
    panels = lax.axis_size("panel")
    myself = lax.axis_index("front")
    place = myself.astype(jnp.int32).reshape(1)
    masks = cube_masks(fronts)
    span = offsets(masks)
    def edge(value):
        return value[leaf_order - iface_rows :]

    sources = leaf_sources[0, 0]
    partial_solution = product(inverse, sources[0])
    update = product(upward, partial_solution)
    held = spread({0: update}, masks)
    parent_high, parent_low = halves(parent_inv[0, 0])

    later = jnp.concatenate([sources[tick] for tick in range(1, ticks)], axis=1)
    along = product(upward, inverse)
    through = jnp.where(lax.axis_index("panel") > 0, product(along, coupling), 0.0)
    next_through = onward(through, -1, 0)
    next_sources = onward(product(along, later), -1, 0)
    next_descended = product(next_through, edge(downward))
    own_later = product(inverse, later)

    tables = (place, parent_of, update_count, row_ids)
    leaf_out = jnp.zeros(sources.shape, jnp.float32)
    parent_out = jnp.zeros(parent_sources.shape[2:], jnp.float32)
    leaf_now = None
    for tick in range(ticks):
        early = {}
        for offset in span[:-1]:
            early[offset] = held[offset]
            early[offset ^ TWIN] = swapped(held[offset], TWIN)
        late = {span[-1]: held[span[-1]], span[-1] ^ TWIN: swapped(held[span[-1]], TWIN)}
        partial_rhs = rows_subtracted(*tables, parent_sources[0, 0], tick, early)
        solved = parent_solve(*tables, parent_high, parent_low, partial_rhs, late)
        other = swapped(solved, TWIN)
        parts = parent_rows(*tables, solved, other, span[-1:])
        parts.update(parent_rows(*tables, after(solved, parts[span[-1]]), other, span[:-1]))
        descended = delivered(parts, masks)
        at = slice((tick - 1) * columns, tick * columns)
        if tick > 0:
            leaving = after(edge(leaf_now), parts[0])
            interface = lax.ppermute(leaving, "panel", [(spot, spot + 1) for spot in range(panels - 1)])
            partial_solution = own_later[:, at] + product(inverse, product(coupling, interface))
        if tick + 1 < ticks:
            at = slice(tick * columns, (tick + 1) * columns)
            base = next_sources[:, at] + product(next_through, edge(partial_solution))
            update = base - product(next_descended, descended)
            moved = {offset: onward(update, 1, offset) for offset in masks}
            moved[0] = onward(update, 1, 0)
            held = dict(moved)
            for step, mask in enumerate(masks):
                for offset in offsets(masks[:step]):
                    if offset ^ mask not in held:
                        held[offset ^ mask] = swapped(held[offset], mask)
            leaf_now = partial_solution - product(downward, after(descended, moved[masks[0]]))
        else:
            leaf_now = partial_solution - product(downward, descended)
        leaf_out = lax.dynamic_update_index_in_dim(leaf_out, leaf_now, tick, 0)
        parent_out = lax.dynamic_update_index_in_dim(parent_out, solved, tick, 0)
    return (leaf_out[None, None], parent_out[None, None])


def solution(mesh):
    placed = (
        P("panel", "front", None, None),
        P("panel", "front", None, None),
        P("panel", "front", None, None),
        P("panel", "front", None, None),
        P("panel", "front", None, None),
        P("panel", "front", None, None, None),
        P("panel", "front", None, None, None),
        P("panel", None),
        P("panel", None),
        P("panel", None, None),
    )
    return jax.shard_map(
        local,
        mesh=mesh,
        in_specs=placed,
        out_specs=(P("panel", "front", None, None, None), P("panel", "front", None, None, None)),
        check_vma=False,
    )
```

```python
import functools

import jax
import jax.numpy as jnp
from jax import lax
from jax.experimental import pallas as pl
from jax.experimental.pallas import tpu as pltpu
from jax.sharding import PartitionSpec as P

TWIN = 1
VMEM_BYTES = 48 * 1024 * 1024


def swapped(value, mask):
    count = lax.axis_size("front")
    return lax.ppermute(value, "front", [(place, place ^ mask) for place in range(count)])


def onward(value, panel_step, mask):
    panels = lax.axis_size("panel")
    fronts = lax.axis_size("front")
    pairs = []
    for panel in range(panels):
        for place in range(fronts):
            goal = (panel + panel_step) % panels
            pairs.append((panel * fronts + place, goal * fronts + (place ^ mask)))
    return lax.ppermute(value, ("panel", "front"), pairs)


def cube_masks(count):
    masks = []
    low = 2
    while low < count:
        masks.append(2 * low - 2)
        low *= 2
    return masks[::-1]


def offsets(masks):
    held = [0]
    for mask in masks:
        held = held + [offset ^ mask for offset in held]
    return held


def spread(held, masks):
    held = dict(held)
    for mask in masks:
        held.update({offset ^ mask: swapped(value, mask) for offset, value in list(held.items())})
    return held


def delivered(parts, masks):
    parts = dict(parts)
    span = offsets(masks)
    for step in range(len(masks) - 1, -1, -1):
        mask = masks[step]
        for offset in span[2 ** step - 1 :: -1]:
            parts[offset] = parts[offset] + swapped(parts.pop(offset ^ mask), mask)
    return parts[0]


def product(matrix, operand):
    return jnp.dot(matrix, operand, precision=lax.Precision.HIGH, preferred_element_type=jnp.float32)


def halves(value):
    rounded = lax.reduce_precision(value, 8, 7)
    return rounded.astype(jnp.bfloat16), (value - rounded).astype(jnp.bfloat16)


def side_by_side(value):
    high = value.astype(jnp.bfloat16)
    low = (value - high.astype(jnp.float32)).astype(jnp.bfloat16)
    return jnp.concatenate([high, low], axis=1)


def summed(pair):
    columns = pair.shape[1] // 2
    return pair[:, :columns] + pair[:, columns:]


def after(value, event):
    return lax.optimization_barrier((value, event))[0]


def subtract_rows(rhs, offsets_in, blocks, place, parents, counts, rows):
    cap = rows.shape[1]
    extent = (rhs.shape[0], cap)
    for offset, block in zip(offsets_in, blocks):
        leaf = place[0] ^ offset

        @pl.when(parents[0, leaf] == place[0])
        def _():
            slot = lax.broadcasted_iota(jnp.int32, (1, cap), 1)
            targets = jnp.where(slot < counts[0, leaf], rows[pl.ds(leaf, 1), :], -1)
            choice = lax.broadcasted_iota(jnp.int32, extent, 0) == targets
            pair = jnp.dot(
                jnp.where(choice, 1.0, 0.0).astype(jnp.bfloat16),
                side_by_side(block[...]),
                preferred_element_type=jnp.float32,
            )
            rhs[...] -= summed(pair)


def early_kernel(offsets_in, tick, place, parents, counts, rows, sources, *refs):
    blocks, rhs = refs[:-1], refs[-1]
    rhs[...] = sources[tick]
    subtract_rows(rhs, offsets_in, blocks, place, parents, counts, rows)


def solve_kernel(offsets_in, place, parents, counts, rows, high, low, partial_rhs, *refs):
    blocks, out, rhs = refs[:-2], refs[-2], refs[-1]
    rhs[...] = partial_rhs[...]
    subtract_rows(rhs, offsets_in, blocks, place, parents, counts, rows)
    both = side_by_side(rhs[...])
    columns = out.shape[1]
    out[...] = summed(jnp.dot(high[...], both, preferred_element_type=jnp.float32)) + jnp.dot(
        low[...], both[:, :columns], preferred_element_type=jnp.float32
    )


def rows_subtracted(place, parents, counts, rows, sources, tick, blocks):
    smem = pl.BlockSpec(memory_space=pltpu.SMEM)
    vmem = pl.BlockSpec(memory_space=pltpu.VMEM)
    order, columns = sources.shape[1:]
    return pl.pallas_call(
        functools.partial(early_kernel, list(blocks), tick),
        out_shape=jax.ShapeDtypeStruct((order, columns), jnp.float32),
        in_specs=[smem] * 3 + [vmem] * (2 + len(blocks)),
        out_specs=vmem,
        compiler_params=pltpu.CompilerParams(vmem_limit_bytes=VMEM_BYTES),
        cost_estimate=pl.CostEstimate(flops=1000, bytes_accessed=1000, transcendentals=0),
        name="rows_subtracted",
    )(place, parents, counts, rows, sources, *blocks.values())


def parent_solve(place, parents, counts, rows, high, low, partial_rhs, blocks):
    order, columns = partial_rhs.shape
    smem = pl.BlockSpec(memory_space=pltpu.SMEM)
    vmem = pl.BlockSpec(memory_space=pltpu.VMEM)
    return pl.pallas_call(
        functools.partial(solve_kernel, list(blocks)),
        out_shape=jax.ShapeDtypeStruct(partial_rhs.shape, jnp.float32),
        in_specs=[smem] * 3 + [vmem] * (4 + len(blocks)),
        out_specs=vmem,
        scratch_shapes=[pltpu.VMEM(partial_rhs.shape, jnp.float32)],
        compiler_params=pltpu.CompilerParams(vmem_limit_bytes=VMEM_BYTES),
        cost_estimate=pl.CostEstimate(flops=1000, bytes_accessed=1000, transcendentals=0),
        name="parent_solve",
    )(place, parents, counts, rows, high, low, partial_rhs, *blocks.values())


def rows_kernel(offsets_out, place, parents, counts, rows, own, other, *refs):
    outs, wide = refs[:-1], refs[-1]
    wide[0] = side_by_side(own[...])
    wide[1] = side_by_side(other[...])
    cap = rows.shape[1]
    order = own.shape[0]
    lanes = 128
    for offset, out in zip(offsets_out, outs):
        leaf = place[0] ^ offset
        parent = parents[0, leaf]
        mine = parent == place[0]
        here = mine | (parent == (place[0] ^ TWIN))

        @pl.when(jnp.logical_not(here))
        def _():
            out[...] = jnp.zeros_like(out)

        @pl.when(here)
        def _():
            slot = lax.broadcasted_iota(jnp.int32, (lanes, cap), 1)
            column = jnp.where(slot < counts[0, leaf], jnp.broadcast_to(rows[pl.ds(leaf, 1), :], (lanes, cap)), -1).T
            lane = lax.broadcasted_iota(jnp.int32, (cap, lanes), 1)
            choice = jnp.concatenate(
                [jnp.where(column == lane + start, 1.0, 0.0).astype(jnp.bfloat16) for start in range(0, order, lanes)],
                axis=1,
            )
            out[...] = summed(
                jnp.dot(choice, wide[jnp.where(mine, 0, 1)], preferred_element_type=jnp.float32)
            )


def parent_rows(place, parents, counts, rows, own, other, wanted):
    cap = rows.shape[1]
    order, columns = own.shape
    smem = pl.BlockSpec(memory_space=pltpu.SMEM)
    vmem = pl.BlockSpec(memory_space=pltpu.VMEM)
    found = pl.pallas_call(
        functools.partial(rows_kernel, wanted),
        out_shape=[jax.ShapeDtypeStruct((cap, columns), jnp.float32)] * len(wanted),
        in_specs=[smem] * 3 + [vmem] * 3,
        out_specs=[vmem] * len(wanted),
        scratch_shapes=[pltpu.VMEM((2, order, 2 * columns), jnp.bfloat16)],
        compiler_params=pltpu.CompilerParams(vmem_limit_bytes=VMEM_BYTES),
        cost_estimate=pl.CostEstimate(flops=1000, bytes_accessed=1000, transcendentals=0),
        name="parent_rows",
    )(place, parents, counts, rows, own, other)
    return dict(zip(wanted, found))


def split_product(matrix, wide, columns):
    high = matrix.astype(jnp.bfloat16)
    low = (matrix - high.astype(jnp.float32)).astype(jnp.bfloat16)
    return summed(jnp.dot(high, wide, preferred_element_type=jnp.float32)) + jnp.dot(
        low, wide[:, :columns], preferred_element_type=jnp.float32
    )


def last_kernel(tick, downward, partial_solution, descended, earlier, out, result, sent):
    del earlier
    columns = result.shape[1]
    result[...] = partial_solution[...] - split_product(downward[...], side_by_side(descended[...]), columns)
    copy = pltpu.make_async_copy(result, out.at[tick], sent)
    copy.start()
    copy.wait()


def last_leaf(downward, partial_solution, descended, earlier, tick):
    vmem = pl.BlockSpec(memory_space=pltpu.VMEM)
    return pl.pallas_call(
        functools.partial(last_kernel, tick),
        out_shape=jax.ShapeDtypeStruct(earlier.shape, jnp.float32),
        in_specs=[vmem] * 3 + [pl.BlockSpec(memory_space=pl.ANY)],
        out_specs=pl.BlockSpec(memory_space=pl.ANY),
        scratch_shapes=[pltpu.VMEM(partial_solution.shape, jnp.float32), pltpu.SemaphoreType.DMA],
        input_output_aliases={3: 0},
        compiler_params=pltpu.CompilerParams(vmem_limit_bytes=VMEM_BYTES),
        cost_estimate=pl.CostEstimate(flops=1000, bytes_accessed=1000, transcendentals=0),
        name="last_leaf",
    )(downward, partial_solution, descended, earlier)


def local(
    leaf_inv,
    parent_inv,
    up_coupling,
    down_coupling,
    interface_coupling,
    leaf_sources,
    parent_sources,
    parent_of,
    update_count,
    update_rows,
):
    inverse = leaf_inv[0, 0]
    upward = up_coupling[0, 0]
    downward = down_coupling[0, 0]
    coupling = interface_coupling[0, 0]
    ticks = leaf_sources.shape[2]
    columns = leaf_sources.shape[4]
    leaf_order = inverse.shape[0]
    iface_rows = coupling.shape[1]
    row_ids = update_rows[0]
    fronts = lax.axis_size("front")
    panels = lax.axis_size("panel")
    myself = lax.axis_index("front")
    place = myself.astype(jnp.int32).reshape(1)
    masks = cube_masks(fronts)
    span = offsets(masks)
    def edge(value):
        return value[leaf_order - iface_rows :]

    sources = leaf_sources[0, 0]
    partial_solution = product(inverse, sources[0])
    update = product(upward, partial_solution)
    parent_high, parent_low = halves(parent_inv[0, 0])

    later = jnp.concatenate([sources[tick] for tick in range(1, ticks)], axis=1)
    along = product(upward, inverse)
    through = jnp.where(lax.axis_index("panel") > 0, product(along, coupling), 0.0)
    own_later = product(inverse, later)
    held = spread({0: update}, masks)
    next_through = onward(through, -1, 0)
    next_sources = onward(product(along, later), -1, 0)

    tables = (place, parent_of, update_count, row_ids)
    leaf_out = jnp.zeros(sources.shape, jnp.float32)
    parent_out = jnp.zeros(parent_sources.shape[2:], jnp.float32)
    leaf_now = None
    for tick in range(ticks):
        early = {}
        for offset in span[:-1]:
            early[offset] = held[offset]
            early[offset ^ TWIN] = swapped(held[offset], TWIN)
        late = {span[-1]: held[span[-1]], span[-1] ^ TWIN: swapped(held[span[-1]], TWIN)}
        partial_rhs = rows_subtracted(*tables, parent_sources[0, 0], tick, early)
        solved = parent_solve(*tables, parent_high, parent_low, partial_rhs, late)
        other = swapped(solved, TWIN)
        parts = parent_rows(*tables, solved, other, span[-1:])
        first = (parts[span[-1]], own_later) if tick == 0 else parts[span[-1]]
        parts.update(parent_rows(*tables, after(solved, first), other, span[:-1]))
        descended = delivered(parts, masks)
        if tick == 0:
            next_through = after(next_through, parts[0])
            next_descended = product(next_through, edge(downward))
        at = slice((tick - 1) * columns, tick * columns)
        if tick > 0:
            leaving = after(edge(leaf_now), parts[span[-1]])
            interface = lax.ppermute(leaving, "panel", [(spot, spot + 1) for spot in range(panels - 1)])
            partial_solution = own_later[:, at] + product(inverse, product(coupling, interface))
        if tick + 1 < ticks:
            at = slice(tick * columns, (tick + 1) * columns)
            base = next_sources[:, at] + product(next_through, edge(partial_solution))
            update = base - product(next_descended, descended)
            moved = {offset: onward(update, 1, offset) for offset in (*masks, 0)}
            held = dict(moved)
            for step, mask in enumerate(masks):
                for offset in offsets(masks[:step]):
                    if offset ^ mask not in held:
                        held[offset ^ mask] = swapped(held[offset], mask)
            leaf_now = partial_solution - product(downward, after(descended, moved[masks[0]]))
            leaf_out = lax.dynamic_update_index_in_dim(leaf_out, leaf_now, tick, 0)
        else:
            leaf_out = last_leaf(downward, partial_solution, descended, leaf_out, tick)
        parent_out = lax.dynamic_update_index_in_dim(parent_out, solved, tick, 0)
    return (leaf_out[None, None], parent_out[None, None])


def solution(mesh):
    placed = (
        P("panel", "front", None, None),
        P("panel", "front", None, None),
        P("panel", "front", None, None),
        P("panel", "front", None, None),
        P("panel", "front", None, None),
        P("panel", "front", None, None, None),
        P("panel", "front", None, None, None),
        P("panel", None),
        P("panel", None),
        P("panel", None, None),
    )
    return jax.shard_map(
        local,
        mesh=mesh,
        in_specs=placed,
        out_specs=(P("panel", "front", None, None, None), P("panel", "front", None, None, None)),
        check_vma=False,
    )
```

```python
import functools

import jax
import jax.numpy as jnp
from jax import lax
from jax.experimental import pallas as pl
from jax.experimental.pallas import tpu as pltpu
from jax.sharding import PartitionSpec as P

TWIN = 1
VMEM_BYTES = 48 * 1024 * 1024


def swapped(value, mask):
    count = lax.axis_size("front")
    return lax.ppermute(value, "front", [(place, place ^ mask) for place in range(count)])


def onward(value, panel_step, mask):
    panels = lax.axis_size("panel")
    fronts = lax.axis_size("front")
    pairs = []
    for panel in range(panels):
        for place in range(fronts):
            goal = (panel + panel_step) % panels
            pairs.append((panel * fronts + place, goal * fronts + (place ^ mask)))
    return lax.ppermute(value, ("panel", "front"), pairs)


def cube_masks(count):
    masks = []
    low = 2
    while low < count:
        masks.append(2 * low - 2)
        low *= 2
    return masks[::-1]


def offsets(masks):
    held = [0]
    for mask in masks:
        held = held + [offset ^ mask for offset in held]
    return held


def spread(held, masks):
    held = dict(held)
    for mask in masks:
        held.update({offset ^ mask: swapped(value, mask) for offset, value in list(held.items())})
    return held


def delivered(parts, masks):
    parts = dict(parts)
    span = offsets(masks)
    for step in range(len(masks) - 1, -1, -1):
        mask = masks[step]
        for offset in span[2 ** step - 1 :: -1]:
            parts[offset] = parts[offset] + swapped(parts.pop(offset ^ mask), mask)
    return parts[0]


def product(matrix, operand):
    return jnp.dot(matrix, operand, precision=lax.Precision.HIGH, preferred_element_type=jnp.float32)


def halves(value):
    rounded = lax.reduce_precision(value, 8, 7)
    return rounded.astype(jnp.bfloat16), (value - rounded).astype(jnp.bfloat16)


def side_by_side(value):
    high = value.astype(jnp.bfloat16)
    low = (value - high.astype(jnp.float32)).astype(jnp.bfloat16)
    return jnp.concatenate([high, low], axis=1)


def summed(pair):
    columns = pair.shape[1] // 2
    return pair[:, :columns] + pair[:, columns:]


def after(value, event):
    return lax.optimization_barrier((value, event))[0]


def subtract_rows(rhs, offsets_in, blocks, place, parents, counts, rows):
    cap = rows.shape[1]
    extent = (rhs.shape[0], cap)
    for offset, block in zip(offsets_in, blocks):
        leaf = place[0] ^ offset

        @pl.when(parents[0, leaf] == place[0])
        def _():
            slot = lax.broadcasted_iota(jnp.int32, (1, cap), 1)
            targets = jnp.where(slot < counts[0, leaf], rows[pl.ds(leaf, 1), :], -1)
            choice = lax.broadcasted_iota(jnp.int32, extent, 0) == targets
            pair = jnp.dot(
                jnp.where(choice, 1.0, 0.0).astype(jnp.bfloat16),
                side_by_side(block[...]),
                preferred_element_type=jnp.float32,
            )
            rhs[...] -= summed(pair)


def early_kernel(offsets_in, tick, place, parents, counts, rows, sources, *refs):
    blocks, rhs = refs[:-1], refs[-1]
    rhs[...] = sources[tick]
    subtract_rows(rhs, offsets_in, blocks, place, parents, counts, rows)


def solve_kernel(offsets_in, place, parents, counts, rows, high, low, partial_rhs, *refs):
    blocks, out, rhs = refs[:-2], refs[-2], refs[-1]
    rhs[...] = partial_rhs[...]
    subtract_rows(rhs, offsets_in, blocks, place, parents, counts, rows)
    both = side_by_side(rhs[...])
    columns = out.shape[1]
    out[...] = summed(jnp.dot(high[...], both, preferred_element_type=jnp.float32)) + jnp.dot(
        low[...], both[:, :columns], preferred_element_type=jnp.float32
    )


def rows_subtracted(place, parents, counts, rows, sources, tick, blocks):
    smem = pl.BlockSpec(memory_space=pltpu.SMEM)
    vmem = pl.BlockSpec(memory_space=pltpu.VMEM)
    order, columns = sources.shape[1:]
    return pl.pallas_call(
        functools.partial(early_kernel, list(blocks), tick),
        out_shape=jax.ShapeDtypeStruct((order, columns), jnp.float32),
        in_specs=[smem] * 3 + [vmem] * (2 + len(blocks)),
        out_specs=vmem,
        compiler_params=pltpu.CompilerParams(vmem_limit_bytes=VMEM_BYTES),
        cost_estimate=pl.CostEstimate(flops=1000, bytes_accessed=1000, transcendentals=0),
        name="rows_subtracted",
    )(place, parents, counts, rows, sources, *blocks.values())


def parent_solve(place, parents, counts, rows, high, low, partial_rhs, blocks):
    order, columns = partial_rhs.shape
    smem = pl.BlockSpec(memory_space=pltpu.SMEM)
    vmem = pl.BlockSpec(memory_space=pltpu.VMEM)
    return pl.pallas_call(
        functools.partial(solve_kernel, list(blocks)),
        out_shape=jax.ShapeDtypeStruct(partial_rhs.shape, jnp.float32),
        in_specs=[smem] * 3 + [vmem] * (4 + len(blocks)),
        out_specs=vmem,
        scratch_shapes=[pltpu.VMEM(partial_rhs.shape, jnp.float32)],
        compiler_params=pltpu.CompilerParams(vmem_limit_bytes=VMEM_BYTES),
        cost_estimate=pl.CostEstimate(flops=1000, bytes_accessed=1000, transcendentals=0),
        name="parent_solve",
    )(place, parents, counts, rows, high, low, partial_rhs, *blocks.values())


def rows_kernel(offsets_out, place, parents, counts, rows, own, other, *refs):
    outs, wide = refs[:-1], refs[-1]
    wide[0] = side_by_side(own[...])
    wide[1] = side_by_side(other[...])
    cap = rows.shape[1]
    order = own.shape[0]
    lanes = 128
    for offset, out in zip(offsets_out, outs):
        leaf = place[0] ^ offset
        parent = parents[0, leaf]
        mine = parent == place[0]
        here = mine | (parent == (place[0] ^ TWIN))

        @pl.when(jnp.logical_not(here))
        def _():
            out[...] = jnp.zeros_like(out)

        @pl.when(here)
        def _():
            slot = lax.broadcasted_iota(jnp.int32, (lanes, cap), 1)
            column = jnp.where(slot < counts[0, leaf], jnp.broadcast_to(rows[pl.ds(leaf, 1), :], (lanes, cap)), -1).T
            lane = lax.broadcasted_iota(jnp.int32, (cap, lanes), 1)
            choice = jnp.concatenate(
                [jnp.where(column == lane + start, 1.0, 0.0).astype(jnp.bfloat16) for start in range(0, order, lanes)],
                axis=1,
            )
            out[...] = summed(
                jnp.dot(choice, wide[jnp.where(mine, 0, 1)], preferred_element_type=jnp.float32)
            )


def parent_rows(place, parents, counts, rows, own, other, wanted):
    cap = rows.shape[1]
    order, columns = own.shape
    smem = pl.BlockSpec(memory_space=pltpu.SMEM)
    vmem = pl.BlockSpec(memory_space=pltpu.VMEM)
    found = pl.pallas_call(
        functools.partial(rows_kernel, wanted),
        out_shape=[jax.ShapeDtypeStruct((cap, columns), jnp.float32)] * len(wanted),
        in_specs=[smem] * 3 + [vmem] * 3,
        out_specs=[vmem] * len(wanted),
        scratch_shapes=[pltpu.VMEM((2, order, 2 * columns), jnp.bfloat16)],
        compiler_params=pltpu.CompilerParams(vmem_limit_bytes=VMEM_BYTES),
        cost_estimate=pl.CostEstimate(flops=1000, bytes_accessed=1000, transcendentals=0),
        name="parent_rows",
    )(place, parents, counts, rows, own, other)
    return dict(zip(wanted, found))


def local(
    leaf_inv,
    parent_inv,
    up_coupling,
    down_coupling,
    interface_coupling,
    leaf_sources,
    parent_sources,
    parent_of,
    update_count,
    update_rows,
):
    inverse = leaf_inv[0, 0]
    upward = up_coupling[0, 0]
    downward = down_coupling[0, 0]
    coupling = interface_coupling[0, 0]
    ticks = leaf_sources.shape[2]
    columns = leaf_sources.shape[4]
    leaf_order = inverse.shape[0]
    iface_rows = coupling.shape[1]
    row_ids = update_rows[0]
    fronts = lax.axis_size("front")
    panels = lax.axis_size("panel")
    myself = lax.axis_index("front")
    place = myself.astype(jnp.int32).reshape(1)
    masks = cube_masks(fronts)
    span = offsets(masks)

    def edge(value):
        return value[leaf_order - iface_rows :]

    sources = leaf_sources[0, 0]
    partial_solution = product(inverse, sources[0])
    update = product(upward, partial_solution)
    parent_high, parent_low = halves(parent_inv[0, 0])

    later = jnp.concatenate([sources[tick] for tick in range(1, ticks)], axis=1)
    along = product(upward, inverse)
    through = jnp.where(lax.axis_index("panel") > 0, product(along, coupling), 0.0)
    own_later = product(inverse, later)
    held = spread({0: update}, masks)
    next_through = onward(through, -1, 0)
    next_sources = onward(product(along, later), -1, 0)

    tables = (place, parent_of, update_count, row_ids)
    leaf_out = jnp.zeros(sources.shape, jnp.float32)
    parent_out = jnp.zeros(parent_sources.shape[2:], jnp.float32)
    leaf_now = None
    for tick in range(ticks):
        early = {}
        for offset in span[:-1]:
            early[offset] = held[offset]
            early[offset ^ TWIN] = swapped(held[offset], TWIN)
        late = {span[-1]: held[span[-1]], span[-1] ^ TWIN: swapped(held[span[-1]], TWIN)}
        partial_rhs = rows_subtracted(*tables, parent_sources[0, 0], tick, early)
        solved = parent_solve(*tables, parent_high, parent_low, partial_rhs, late)
        other = swapped(solved, TWIN)
        parts = parent_rows(*tables, solved, other, span[-1:])
        first = (parts[span[-1]], own_later) if tick == 0 else parts[span[-1]]
        parts.update(parent_rows(*tables, after(solved, first), other, span[:-1]))
        descended = delivered(parts, masks)
        if tick == 0:
            next_through = after(next_through, parts[0])
            next_descended = product(next_through, edge(downward))
        at = slice((tick - 1) * columns, tick * columns)
        if tick > 0:
            leaving = after(edge(leaf_now), parts[span[-1]])
            interface = lax.ppermute(leaving, "panel", [(spot, spot + 1) for spot in range(panels - 1)])
            partial_solution = own_later[:, at] + product(inverse, product(coupling, interface))
        if tick + 1 < ticks:
            at = slice(tick * columns, (tick + 1) * columns)
            base = next_sources[:, at] + product(next_through, edge(partial_solution))
            update = base - product(next_descended, descended)
            moved = {offset: onward(update, 1, offset) for offset in (*masks, 0)}
            held = dict(moved)
            for step, mask in enumerate(masks):
                for offset in offsets(masks[:step]):
                    if offset ^ mask not in held:
                        held[offset ^ mask] = swapped(held[offset], mask)
            leaf_now = partial_solution - product(downward, after(descended, moved[masks[0]]))
        else:
            leaf_now = partial_solution - product(downward, descended)
        leaf_out = lax.dynamic_update_index_in_dim(leaf_out, leaf_now, tick, 0)
        parent_out = lax.dynamic_update_index_in_dim(parent_out, solved, tick, 0)
    return (leaf_out[None, None], parent_out[None, None])


def solution(mesh):
    placed = (
        P("panel", "front", None, None),
        P("panel", "front", None, None),
        P("panel", "front", None, None),
        P("panel", "front", None, None),
        P("panel", "front", None, None),
        P("panel", "front", None, None, None),
        P("panel", "front", None, None, None),
        P("panel", None),
        P("panel", None),
        P("panel", None, None),
    )
    return jax.shard_map(
        local,
        mesh=mesh,
        in_specs=placed,
        out_specs=(P("panel", "front", None, None, None), P("panel", "front", None, None, None)),
        check_vma=False,
    )
```
